256 devices in a mesh: section: 4 (over x_hi, core), ctx: 64 (over x_lo, y, z).
Axes of the slice: x: 4 (x_hi: 2, x_lo: 2; x = x_hi * 2 + x_lo), y: 4, z: 8, core: 2. Of those that a mesh axis runs over, the one named last changes fastest.
Arguments:
- grad_next: bfloat16 [4, 8192, 4096], P('section', 'ctx'), may hold values from -0.0625 to 0.0625
- gate: bfloat16 [4, 8192, 4096], P('section', 'ctx'), may hold values from -6 to 6
- conv_input: bfloat16 [4, 8192, 4096], P('section', 'ctx'), may hold values from -6 to 6
- saved_conv: bfloat16 [4, 8192, 4096], P('section', 'ctx'), may hold values from -320 to 320
- long_filter: bfloat16 [4, 8192, 4096], P('section', 'ctx'), may hold values from -16 to 16
Outputs:
- grad_input: bfloat16 [4, 8192, 4096], P('section', 'ctx')
- grad_gate: bfloat16 [4, 8192, 4096], P('section', 'ctx')
- filter_grad: bfloat16 [4, 8192, 4096], P('section', 'ctx')
The draws below stay inside these ranges and needn't reach their ends.
All inputs are finite; a program needn't handle non-finite values.
Results may differ from the reference program's by a relative error of at most 0.0095.
Values may be sent and summed in bfloat16 or wider, within the bound.
A program may use at most 192 MiB of HBM per device.

```python
import math
import jax
import jax.numpy as jnp
from jax import lax

C = 4096
TOK_DEV = 128
TOKENS = 8192
LAYERS = 4
N_CTX = 64


def draw_saved_conv(key, part):
    key = jax.random.fold_in(key, 12)
    values = jax.random.truncated_normal(key, -5.0, 5.0, (LAYERS, TOKENS, C), jnp.float32)
    return (values * 64.0).astype(jnp.bfloat16)


def draw_long_filter(key, part):
    key = jax.random.fold_in(key, 11)
    rate_key, noise_key = jax.random.split(key)
    lowest = math.log(1.0 / (32.0 * TOKENS))
    highest = math.log(1.0 / 30.0)
    noise = jax.random.truncated_normal(noise_key, -4.0, 4.0, (LAYERS, TOKENS, C), jnp.float32)
    rates = jnp.exp(jax.random.uniform(rate_key, (LAYERS, 1, C), jnp.float32, lowest, highest))
    lags = jnp.arange(TOKENS, dtype=jnp.float32)[None, :, None]
    norms = jnp.sqrt(TOKENS * -jnp.expm1(-2.0 * rates) / -jnp.expm1(-2.0 * rates * TOKENS))
    return jnp.clip(noise * jnp.exp(-rates * lags) * norms, -16.0, 16.0).astype(jnp.bfloat16)


def shard_levels(key, shape, shards, low, top_value):
    loudness, own = 1.0, jax.random.fold_in(key, 6)
    for axis_at, shards_of in shards:
        heights = jnp.exp(jax.random.uniform(jax.random.fold_in(own, axis_at), (shards_of,), jnp.float32, low / len(shards), top_value / len(shards)))
        loudness = loudness * jnp.repeat(heights, shape[axis_at] // shards_of).reshape([-1 if axis == axis_at else 1 for axis in range(len(shape))])
    return loudness


def scatter_about(own_key, dims, spread, limit, cuts=(), held_as=jnp.bfloat16):
    values = spread * jax.random.normal(own_key, dims, jnp.float32)
    if cuts:
        values = values * shard_levels(own_key, dims, cuts, -0.22, 0.18)
    return jnp.clip(values, -limit, limit).astype(held_as)


def setup_inputs(seed: int = 0) -> dict:
    arg_keys = jax.random.split(jax.random.key(seed), 6)
    return {
        "grad_next": scatter_about(arg_keys[0], (LAYERS, TOKENS, C), TOKENS ** -0.5, 0.0625, ((0, 4), (1, 64))),
        "gate": scatter_about(arg_keys[1], (LAYERS, TOKENS, C), 1.0, 6.0, ((0, 4), (1, 64))),
        "conv_input": scatter_about(arg_keys[2], (LAYERS, TOKENS, C), 1.0, 6.0, ((0, 4), (1, 64))),
        "saved_conv": draw_saved_conv(jax.random.fold_in(arg_keys[5], 71), 0),
        "long_filter": draw_long_filter(jax.random.fold_in(arg_keys[5], 71), 0),
    }


HIGHEST = lax.Precision.HIGHEST


def outer_tables(ctx_count):
    outer_len = 2 * ctx_count
    outer_idx = jnp.arange(outer_len, dtype=jnp.int32)
    positions = jnp.arange(ctx_count, dtype=jnp.int32)
    angle_outer = (2.0 * math.pi / outer_len) * ((outer_idx[:, None] * positions[None, :]) % outer_len).astype(jnp.float32)
    return jnp.cos(angle_outer).astype(jnp.bfloat16), (-jnp.sin(angle_outer)).astype(jnp.bfloat16)


def twisted_rows(rows_k1, block_len, outer_len):
    full_len = outer_len * block_len
    inner_idx = jnp.arange(block_len, dtype=jnp.int32)
    freq = rows_k1[:, None, None] + outer_len * inner_idx[None, :, None]
    angle = (2.0 * math.pi / full_len) * ((inner_idx[None, None, :] * freq) % full_len).astype(jnp.float32)
    return jnp.cos(angle).astype(jnp.bfloat16), (-jnp.sin(angle)).astype(jnp.bfloat16)


def round_half(values):
    return lax.optimization_barrier(values.astype(jnp.bfloat16)).astype(jnp.float32)


def transform(signal, tables, ctx_count, block_len):
    cos_outer, sin_outer, tw_re, tw_im = tables
    shaped = signal.reshape(ctx_count, block_len, -1).astype(jnp.float32)
    first_re = round_half(jnp.einsum('kp,pjw->kjw', cos_outer.astype(jnp.float32), shaped, precision=HIGHEST))
    first_im = round_half(jnp.einsum('kp,pjw->kjw', sin_outer.astype(jnp.float32), shaped, precision=HIGHEST))
    spec_re = (jnp.einsum('kqj,kjw->kqw', tw_re, first_re, precision=HIGHEST)
               - jnp.einsum('kqj,kjw->kqw', tw_im, first_im, precision=HIGHEST))
    spec_im = (jnp.einsum('kqj,kjw->kqw', tw_re, first_im, precision=HIGHEST)
               + jnp.einsum('kqj,kjw->kqw', tw_im, first_re, precision=HIGHEST))
    return spec_re, spec_im


def restore(cross_re, cross_im, tables, ctx_count, block_len):
    cos_outer, sin_outer, tw_re, tw_im = tables
    full_len = 2 * ctx_count * block_len
    turned_re = round_half(jnp.einsum('kqj,kqw->kjw', tw_re, cross_re, precision=HIGHEST)
                           + jnp.einsum('kqj,kqw->kjw', tw_im, cross_im, precision=HIGHEST))
    turned_im = round_half(jnp.einsum('kqj,kqw->kjw', tw_re, cross_im, precision=HIGHEST)
                           - jnp.einsum('kqj,kqw->kjw', tw_im, cross_re, precision=HIGHEST))
    summed = (jnp.einsum('kp,kjw->pjw', cos_outer.astype(jnp.float32), turned_re, precision=HIGHEST)
              + jnp.einsum('kp,kjw->pjw', sin_outer.astype(jnp.float32), turned_im, precision=HIGHEST))
    channels = cross_re.shape[2]
    return (summed * (1.0 / full_len)).reshape(-1, channels).astype(jnp.bfloat16)


def layer_block(grad_out, gate, conv_input, saved_conv, long_filter, tables, ctx_count, block_len):
    grad_gate = (grad_out.astype(jnp.float32) * saved_conv.astype(jnp.float32)).astype(jnp.bfloat16)
    grad_conv = (grad_out.astype(jnp.float32) * gate.astype(jnp.float32)).astype(jnp.bfloat16)
    input_re, input_im = transform(conv_input, tables, ctx_count, block_len)
    grad_re, grad_im = transform(grad_conv, tables, ctx_count, block_len)
    filt_re, filt_im = transform(long_filter, tables, ctx_count, block_len)
    cross_in_re = round_half(grad_re * filt_re + grad_im * filt_im)
    cross_in_im = round_half(grad_im * filt_re - grad_re * filt_im)
    cross_fi_re = round_half(grad_re * input_re + grad_im * input_im)
    cross_fi_im = round_half(grad_im * input_re - grad_re * input_im)
    grad_input = restore(cross_in_re, cross_in_im, tables, ctx_count, block_len)
    filter_grad = restore(cross_fi_re, cross_fi_im, tables, ctx_count, block_len)
    return grad_input, grad_gate, filter_grad


def reference(grad_next, gate, conv_input, saved_conv, long_filter):
    cos_outer, sin_outer = outer_tables(N_CTX)
    tw_re, tw_im = twisted_rows(jnp.arange(2 * N_CTX, dtype=jnp.int32), TOK_DEV, 2 * N_CTX)
    tables = (cos_outer, sin_outer, tw_re.astype(jnp.float32), tw_im.astype(jnp.float32))
    grad_out = jnp.roll(grad_next, -1, axis=0)
    group_width = math.gcd(C, 256)
    group_count = C // group_width

    def split_up(array):
        return array.reshape(LAYERS, TOKENS, group_count, group_width).transpose(0, 2, 1, 3).reshape(LAYERS * group_count, TOKENS, group_width)

    def join_up(array):
        return array.reshape(LAYERS, group_count, TOKENS, group_width).transpose(0, 2, 1, 3).reshape(LAYERS, TOKENS, C)

    def one_group(operands):
        return layer_block(operands[0], operands[1], operands[2], operands[3], operands[4], tables, N_CTX, TOK_DEV)

    results = lax.map(one_group, (split_up(grad_out), split_up(gate), split_up(conv_input), split_up(saved_conv), split_up(long_filter)))
    return join_up(results[0]), join_up(results[1]), join_up(results[2])
```

```python
import functools
import math

import jax
import jax.numpy as jnp
import numpy as np
from jax import lax
from jax.experimental import pallas as pl
from jax.experimental.pallas import tpu as pltpu
from jax.sharding import PartitionSpec as P

MESH = pl.DeviceIdType.MESH
BF16 = jnp.bfloat16
F32 = jnp.float32

N_CTX = 64
BLOCK = 128
CHANNELS = 4096
HALF = CHANNELS // 2
WIDTH = HALF // N_CTX
OUTER = 2 * N_CTX
FULL = OUTER * BLOCK
SLOTS = N_CTX


def tables():
    k1 = np.arange(N_CTX + 1, dtype=np.int32)
    at = np.arange(N_CTX, dtype=np.int32)
    step = np.float32(2.0 * math.pi / OUTER)
    angle = step * ((k1[:, None] * at[None, :]) % OUTER).astype(np.float32)
    cos = np.cos(angle).astype(jnp.bfloat16).astype(np.float32)
    sin = (-np.sin(angle)).astype(jnp.bfloat16).astype(np.float32)
    rows = np.stack([cos[:N_CTX], sin[:N_CTX]], axis=1)
    rows[0, 1] = cos[N_CTX]
    weight = np.full((SLOTS, 2, 1), 2.0 / FULL, np.float32)
    weight[0] = 1.0 / FULL
    eye = np.eye(8, dtype=np.float32)
    outer_fwd = np.kron(rows.reshape(2 * SLOTS, N_CTX), eye)
    outer_inv = np.kron((rows * weight).reshape(2 * SLOTS, N_CTX).T, eye)
    j = np.arange(BLOCK, dtype=np.int32)
    freq = k1[:, None, None] + OUTER * j[None, :, None]
    step = np.float32(2.0 * math.pi / FULL)
    angle = step * ((j[None, None, :] * freq) % FULL).astype(np.float32)
    re, im = np.cos(angle), -np.sin(angle)
    top = np.concatenate([re, -im], axis=2)
    low = np.concatenate([im, re], axis=2)
    twist = np.concatenate([top, low], axis=1)
    twist[0, :, BLOCK:] = 0.0
    twist[N_CTX] = np.concatenate([np.zeros((2 * BLOCK, BLOCK)), np.concatenate([re[N_CTX], im[N_CTX]], axis=0)], axis=1)
    turn = twist.transpose(0, 2, 1)
    return [t.astype(jnp.bfloat16) for t in (outer_fwd, outer_inv, twist, turn)]


def lane_group(shape):
    return lax.broadcasted_iota(jnp.int32, shape, len(shape) - 1) // WIDTH


def pick(groups, parts):
    out = parts[3]
    for g in (2, 1, 0):
        out = jnp.where(groups == g, parts[g], out)
    return out


def rolled(value, shift):
    return value if isinstance(shift, int) and shift % 128 == 0 else pltpu.roll(value, shift % 128 if isinstance(shift, int) else shift, 1)


def pack_signal(src, dst, half, row):
    groups = lane_group((32, 128))

    def body(e, carry):
        cols = pl.ds(pl.multiple_of(half * HALF + e * 128, 128), 128)
        quarters = [src[32 * q : 32 * q + 32, cols].astype(F32) for q in range(4)]
        for g in range(4):
            parts = [rolled(quarters[q], 32 * (q - g)) for q in range(4)]
            dst[4 * e + g, row : row + 32, :] = pick(groups, parts).astype(BF16)
        return carry

    lax.fori_loop(0, 16, body, 0)


def unpack_outputs(src, filter_out, input_out, half):
    groups = lane_group((64, 128))

    def body(e, carry):
        cols = pl.ds(pl.multiple_of(half * HALF + e * 128, 128), 128)
        got = [src[4 * e + g].astype(F32) for g in range(4)]
        for at in range(4):
            parts = [rolled(got[g], 32 * (g - at)) for g in range(4)]
            value = pick(groups, parts).astype(BF16)
            out = (filter_out, input_out)[at % 2]
            out[64 * (at // 2) : 64 * (at // 2) + 64, cols] = value
        return carry

    lax.fori_loop(0, 16, body, 0)


def first_pass(both, grad, outer_fwd, firsts):
    groups = lane_group((N_CTX * 16, 128))

    def body(jb, carry):
        q = jb // 2
        row = pl.multiple_of((jb % 2) * 16, 16)
        take = lambda ref, at: ref[:, pl.ds(at, 16), :].astype(F32).reshape(N_CTX * 16, 128)
        x_in, x_fi, x_gr = take(both, row), take(both, row + 32), take(grad, row)
        shift = 128 - 32 * q
        parts = [
            pltpu.roll(x_in, shift % 128, 1),
            pltpu.roll(x_fi, (shift + 32) % 128, 1),
            pltpu.roll(x_gr, (shift + 64) % 128, 1),
            pltpu.roll(x_gr, (shift + 96) % 128, 1),
        ]
        x = pick(groups, parts).reshape(N_CTX, 16, 128)
        x = jnp.concatenate(
            [x[:, 8 * h : 8 * h + 8].reshape(N_CTX * 8, 128).astype(BF16) for h in range(2)], axis=1
        )
        for mb in range(2):
            y = jnp.dot(outer_fwd[512 * mb : 512 * mb + 512, :], x, preferred_element_type=F32)
            y = jnp.concatenate([y[:, 128 * h : 128 * h + 128].reshape(64, 8, 128) for h in range(2)], axis=1)
            firsts[64 * mb : 64 * mb + 64, pl.ds(pl.multiple_of(jb * 16, 16), 16), :] = y.astype(BF16)
        return carry

    lax.fori_loop(0, 8, body, 0)


def middle_passes(firsts, twist, turn, turned):
    low = lax.broadcasted_iota(jnp.int32, (64, 128), 1) < 64

    def one(k1, slot):
        data = firsts[pl.ds(2 * slot, 2)].reshape(2 * BLOCK, 128)
        spec = jnp.dot(twist[k1], data, preferred_element_type=F32)
        re, im = spec[:BLOCK], spec[BLOCK:]
        grad_re, grad_im = pltpu.roll(re, 64, 1), pltpu.roll(im, 64, 1)
        cross = jnp.concatenate(
            [(grad_re * re + grad_im * im).astype(BF16), (grad_im * re - grad_re * im).astype(BF16)], axis=0
        )
        return jnp.dot(turn[k1], cross, preferred_element_type=F32)

    def keep(slot, value):
        for part in range(2):
            at = part * BLOCK
            both = jnp.where(low, value[at : at + 64], pltpu.roll(value[at + 64 : at + 128], 64, 1))
            turned[2 * slot + part] = both.astype(BF16)

    def body(i, carry):
        for u in range(3):
            slot = 1 + 3 * i + u
            keep(slot, one(slot, slot))
        return carry

    keep(0, one(0, 0) + one(N_CTX, 0))
    lax.fori_loop(0, 21, body, 0)


def last_pass(turned, outer_inv, out):
    def body(jb, carry):
        rows = pl.ds(pl.multiple_of(jb * 16, 16), 16)
        t = turned[:, rows, :].astype(F32)
        t = jnp.concatenate(
            [t[:, 8 * h : 8 * h + 8].reshape(2 * SLOTS * 8, 128).astype(BF16) for h in range(2)], axis=1
        )
        y = jnp.dot(outer_inv[...], t, preferred_element_type=F32)
        y = jnp.concatenate([y[:, 128 * h : 128 * h + 128].reshape(N_CTX, 8, 128) for h in range(2)], axis=1)
        out[:, rows, :] = y.astype(BF16)
        return carry

    lax.fori_loop(0, 4, body, 0)


def kernel(
    grad_next, gate, conv_input, saved_conv, long_filter, outer_fwd_h, outer_inv_h, twist_h, turn_h,
    grad_input, grad_gate, filter_grad,
    v_in, v_fi, v_gate, v_saved, v_grad, v_gg, v_gc, outer_fwd, outer_inv, twist, turn,
    tx_both, tx_grad, rx_both, rx_grad, firsts, turned, tx_out, rx_out, v_gi, v_fg,
    load_sem, table_sem, store_sem, perm_sem, send_sem, recv_sem,
):
    me = lax.axis_index("ctx")
    section = lax.axis_index("section")
    x, y, z = me // 32, (me // 8) % 4, me % 8

    def peer(i):
        px, py, pz = (x + i // 32) % 2, (y + (i // 8) % 4) % 4, (z + i % 8) % 8
        return px * 32 + py * 8 + pz

    loads = [
        pltpu.make_async_copy(src, dst, load_sem.at[i])
        for i, (src, dst) in enumerate(
            [(conv_input, v_in), (long_filter, v_fi), (gate, v_gate), (saved_conv, v_saved)]
        )
    ]
    for load in loads:
        load.start()
    table_loads = [
        pltpu.make_async_copy(src, dst, table_sem.at[i])
        for i, (src, dst) in enumerate(
            [(outer_fwd_h, outer_fwd), (twist_h, twist), (turn_h, turn), (outer_inv_h, outer_inv)]
        )
    ]

    barrier = pltpu.get_barrier_semaphore()

    def greet(i, carry):
        pl.semaphore_signal(barrier, inc=1, device_id={"ctx": peer(i)}, device_id_type=MESH)
        return carry

    pl.semaphore_signal(barrier, inc=1, device_id={"section": (section + 1) % 4}, device_id_type=MESH)
    lax.fori_loop(1, N_CTX, greet, 0)

    loads[0].wait()
    loads[1].wait()
    pack_signal(v_in, tx_both.at[0], 0, 0)
    pack_signal(v_fi, tx_both.at[0], 0, 32)
    pl.semaphore_wait(barrier, N_CTX)

    passed = pltpu.make_async_remote_copy(
        src_ref=grad_next, dst_ref=v_grad, send_sem=perm_sem.at[0], recv_sem=perm_sem.at[1],
        device_id={"section": (section + 3) % 4}, device_id_type=MESH,
    )
    passed.start()

    def send(tx, rx, which):
        pltpu.make_async_copy(tx.at[me], rx.at[me], recv_sem.at[which]).start()

        def body(i, carry):
            d = peer(i)
            pltpu.make_async_remote_copy(
                src_ref=tx.at[d], dst_ref=rx.at[me], send_sem=send_sem.at[which], recv_sem=recv_sem.at[which],
                device_id={"ctx": d}, device_id_type=MESH,
            ).start()
            return carry

        lax.fori_loop(1, N_CTX, body, 0)

    def arrived(rx, which):
        pltpu.make_async_copy(rx, rx, recv_sem.at[which]).wait()

    def sent(tx, which):
        part = tx.at[pl.ds(0, N_CTX - 1)]
        pltpu.make_async_copy(part, part, send_sem.at[which]).wait()

    send(tx_both.at[0], rx_both.at[0], 0)
    for load in table_loads:
        load.start()
    pack_signal(v_in, tx_both.at[1], 1, 0)
    pack_signal(v_fi, tx_both.at[1], 1, 32)
    loads[2].wait()
    loads[3].wait()
    passed.wait_recv()

    def gating(r, carry):
        rows = pl.ds(pl.multiple_of(r * 16, 16), 16)
        grad = v_grad[rows, :].astype(F32)
        v_gc[rows, :] = (grad * v_gate[rows, :].astype(F32)).astype(BF16)
        v_gg[rows, :] = (grad * v_saved[rows, :].astype(F32)).astype(BF16)
        return carry

    lax.fori_loop(0, BLOCK // 16, gating, 0)
    pack_signal(v_gc, tx_grad.at[0], 0, 0)
    send(tx_grad.at[0], rx_grad.at[0], 1)
    send(tx_both.at[1], rx_both.at[1], 2)
    pack_signal(v_gc, tx_grad.at[1], 1, 0)
    send(tx_grad.at[1], rx_grad.at[1], 3)
    stores = [pltpu.make_async_copy(v_gg, grad_gate, store_sem.at[0])]
    stores[0].start()
    for load in table_loads:
        load.wait()

    for half in range(2):
        arrived(rx_both.at[half], 2 * half)
        arrived(rx_grad.at[half], 2 * half + 1)
        first_pass(rx_both.at[half], rx_grad.at[half], outer_fwd, firsts)
        middle_passes(firsts, twist, turn, turned)
        last_pass(turned, outer_inv, tx_out.at[half])
        send(tx_out.at[half], rx_out.at[half], 4 + half)

    for half in range(2):
        arrived(rx_out.at[half], 4 + half)
        unpack_outputs(rx_out.at[half], v_fg, v_gi, half)
        cols = pl.ds(half * HALF, HALF)
        for i, (src, dst) in enumerate([(v_gi, grad_input), (v_fg, filter_grad)]):
            store = pltpu.make_async_copy(src.at[:, cols], dst.at[:, cols], store_sem.at[1 + 2 * half + i])
            store.start()
            stores.append(store)

    passed.wait_send()
    for half in range(2):
        sent(tx_both.at[half], 2 * half)
        sent(tx_grad.at[half], 2 * half + 1)
        sent(tx_out.at[half], 4 + half)
    for store in stores:
        store.wait()


def per_device(consts, grad_next, gate, conv_input, saved_conv, long_filter):
    args = [a[0] for a in (grad_next, gate, conv_input, saved_conv, long_filter)]
    shard = jax.ShapeDtypeStruct((BLOCK, CHANNELS), BF16)
    any_spec = pl.BlockSpec(memory_space=pl.ANY)
    vmem = lambda *shape: pltpu.VMEM(shape, BF16)
    outs = pl.pallas_call(
        kernel,
        out_shape=[shard] * 3,
        in_specs=[any_spec] * 9,
        out_specs=[any_spec] * 3,
        scratch_shapes=[vmem(BLOCK, CHANNELS)] * 7
        + [vmem(*c.shape) for c in consts]
        + [
            vmem(2, N_CTX, 64, 128), vmem(2, N_CTX, 32, 128),
            vmem(2, N_CTX, 64, 128), vmem(2, N_CTX, 32, 128),
            vmem(2 * SLOTS, BLOCK, 128), vmem(2 * SLOTS, 64, 128),
            vmem(2, N_CTX, 64, 128), vmem(2, N_CTX, 64, 128),
            vmem(BLOCK, CHANNELS), vmem(BLOCK, CHANNELS),
            pltpu.SemaphoreType.DMA((4,)), pltpu.SemaphoreType.DMA((4,)), pltpu.SemaphoreType.DMA((5,)),
            pltpu.SemaphoreType.DMA((2,)), pltpu.SemaphoreType.DMA((6,)), pltpu.SemaphoreType.DMA((6,)),
        ],
        compiler_params=pltpu.CompilerParams(
            collective_id=0, has_side_effects=True, vmem_limit_bytes=58 * 2**20
        ),
    )(*args, *consts)
    return tuple(o[None] for o in outs)


def solution(mesh):
    consts = tables()
    spec = P("section", "ctx", None)
    return jax.shard_map(
        functools.partial(per_device, [jnp.asarray(c) for c in consts]),
        mesh=mesh, in_specs=(spec,) * 5, out_specs=(spec,) * 3, check_vma=False,
    )
```

```python
import functools
import math

import jax
import jax.numpy as jnp
import numpy as np
from jax import lax
from jax.experimental import pallas as pl
from jax.experimental.pallas import tpu as pltpu
from jax.sharding import PartitionSpec as P

MESH = pl.DeviceIdType.MESH
BF16 = jnp.bfloat16
F32 = jnp.float32

N_CTX = 64
BLOCK = 128
CHANNELS = 4096
HALF = CHANNELS // 2
WIDTH = HALF // N_CTX
OUTER = 2 * N_CTX
FULL = OUTER * BLOCK
SLOTS = N_CTX


def tables():
    k1 = np.arange(N_CTX + 1, dtype=np.int32)
    at = np.arange(N_CTX, dtype=np.int32)
    step = np.float32(2.0 * math.pi / OUTER)
    angle = step * ((k1[:, None] * at[None, :]) % OUTER).astype(np.float32)
    cos = np.cos(angle).astype(jnp.bfloat16).astype(np.float32)
    sin = (-np.sin(angle)).astype(jnp.bfloat16).astype(np.float32)
    rows = np.stack([cos[:N_CTX], sin[:N_CTX]], axis=1)
    rows[0, 1] = cos[N_CTX]
    weight = np.full((SLOTS, 2, 1), 2.0 / FULL, np.float32)
    weight[0] = 1.0 / FULL
    eye = np.eye(8, dtype=np.float32)
    outer_fwd = np.kron(rows.reshape(2 * SLOTS, N_CTX), eye)
    outer_inv = np.kron((rows * weight).reshape(2 * SLOTS, N_CTX).T, eye)
    j = np.arange(BLOCK, dtype=np.int32)
    freq = k1[:, None, None] + OUTER * j[None, :, None]
    step = np.float32(2.0 * math.pi / FULL)
    angle = step * ((j[None, None, :] * freq) % FULL).astype(np.float32)
    re, im = np.cos(angle), -np.sin(angle)
    top = np.concatenate([re, -im], axis=2)
    low = np.concatenate([im, re], axis=2)
    twist = np.concatenate([top, low], axis=1)
    twist[0, :, BLOCK:] = 0.0
    twist[N_CTX] = np.concatenate([np.zeros((2 * BLOCK, BLOCK)), np.concatenate([re[N_CTX], im[N_CTX]], axis=0)], axis=1)
    turn = twist.transpose(0, 2, 1)
    return [t.astype(jnp.bfloat16) for t in (outer_fwd, outer_inv, twist, turn)]


def lane_group(shape):
    return lax.broadcasted_iota(jnp.int32, shape, len(shape) - 1) // WIDTH


def pick(groups, parts):
    out = parts[3]
    for g in (2, 1, 0):
        out = jnp.where(groups == g, parts[g], out)
    return out


def rolled(value, shift):
    return value if isinstance(shift, int) and shift % 128 == 0 else pltpu.roll(value, shift % 128 if isinstance(shift, int) else shift, 1)


def pack_signal(src, dst, half, row):
    groups = lane_group((32, 128))

    def body(e, carry):
        cols = pl.ds(pl.multiple_of(half * HALF + e * 128, 128), 128)
        quarters = [src[32 * q : 32 * q + 32, cols] for q in range(4)]
        for g in range(4):
            parts = [rolled(quarters[q], 32 * (q - g)) for q in range(4)]
            dst[4 * e + g, row : row + 32, :] = pick(groups, parts)
        return carry

    lax.fori_loop(0, 16, body, 0)


def unpack_outputs(src, filter_out, input_out, first, last):
    groups = lane_group((64, 128))

    def body(e, carry):
        cols = pl.ds(pl.multiple_of(e * 128, 128), 128)
        got = [src[4 * e + g] for g in range(4)]
        for at in range(4):
            parts = [rolled(got[g], 32 * (g - at)) for g in range(4)]
            out = (filter_out, input_out)[at % 2]
            out[64 * (at // 2) : 64 * (at // 2) + 64, cols] = pick(groups, parts)
        return carry

    lax.fori_loop(first, last, body, 0)


def first_pass(both, grad, outer_fwd, firsts):
    groups = lane_group((N_CTX * 16, 128))

    def body(jb, carry):
        q = jb // 2
        row = pl.multiple_of((jb % 2) * 16, 16)
        take = lambda ref, at: ref[:, pl.ds(at, 16), :].astype(F32).reshape(N_CTX * 16, 128)
        x_in, x_fi, x_gr = take(both, row), take(both, row + 32), take(grad, row)
        shift = 128 - 32 * q
        parts = [
            pltpu.roll(x_in, shift % 128, 1),
            pltpu.roll(x_fi, (shift + 32) % 128, 1),
            pltpu.roll(x_gr, (shift + 64) % 128, 1),
            pltpu.roll(x_gr, (shift + 96) % 128, 1),
        ]
        x = pick(groups, parts).reshape(N_CTX, 16, 128)
        x = jnp.concatenate(
            [x[:, 8 * h : 8 * h + 8].reshape(N_CTX * 8, 128).astype(BF16) for h in range(2)], axis=1
        )
        for mb in range(2):
            y = jnp.dot(outer_fwd[512 * mb : 512 * mb + 512, :], x, preferred_element_type=F32)
            y = jnp.concatenate([y[:, 128 * h : 128 * h + 128].reshape(64, 8, 128) for h in range(2)], axis=1)
            firsts[64 * mb : 64 * mb + 64, pl.ds(pl.multiple_of(jb * 16, 16), 16), :] = y.astype(BF16)
        return carry

    lax.fori_loop(0, 8, body, 0)


def middle_passes(firsts, twist, turn, turned):
    low = lax.broadcasted_iota(jnp.int32, (64, 128), 1) < 64

    def spectra(k1, slot):
        data = firsts[pl.ds(2 * slot, 2)].reshape(2 * BLOCK, 128)
        return jnp.dot(twist[k1], data, preferred_element_type=F32)

    def crossed(spec):
        re, im = spec[:BLOCK], spec[BLOCK:]
        grad_re, grad_im = pltpu.roll(re, 64, 1), pltpu.roll(im, 64, 1)
        return jnp.concatenate(
            [(grad_re * re + grad_im * im).astype(BF16), (grad_im * re - grad_re * im).astype(BF16)], axis=0
        )

    def turn_of(k1, cross):
        return jnp.dot(turn[k1], cross, preferred_element_type=F32)

    def keep(slot, value):
        for part in range(2):
            at = part * BLOCK
            both = jnp.where(low, value[at : at + 64], pltpu.roll(value[at + 64 : at + 128], 64, 1))
            turned[2 * slot + part] = both.astype(BF16)

    def body(i, carry):
        slots = [1 + 7 * i + u for u in range(7)]
        specs = [spectra(k, k) for k in slots]
        cross = [crossed(v) for v in specs]
        turns = [turn_of(k, c) for k, c in zip(slots, cross)]
        for k, t in zip(slots, turns):
            keep(k, t)
        return carry

    keep(0, turn_of(0, crossed(spectra(0, 0))) + turn_of(N_CTX, crossed(spectra(N_CTX, 0))))
    lax.fori_loop(0, 9, body, 0)


def last_pass(turned, outer_inv, out):
    def body(jb, carry):
        rows = pl.ds(pl.multiple_of(jb * 16, 16), 16)
        t = turned[:, rows, :].astype(F32)
        t = jnp.concatenate(
            [t[:, 8 * h : 8 * h + 8].reshape(2 * SLOTS * 8, 128).astype(BF16) for h in range(2)], axis=1
        )
        y = jnp.dot(outer_inv[...], t, preferred_element_type=F32)
        y = jnp.concatenate([y[:, 128 * h : 128 * h + 128].reshape(N_CTX, 8, 128) for h in range(2)], axis=1)
        out[:, rows, :] = y.astype(BF16)
        return carry

    lax.fori_loop(0, 4, body, 0)


def kernel(
    grad_next, gate, conv_input, saved_conv, long_filter, outer_fwd_h, outer_inv_h, twist_h, turn_h,
    gg_out, part_out, got,
    v_in, v_fi, v_gate, v_saved, v_grad, v_gg, v_gc, outer_fwd, outer_inv, twist, turn,
    tx_both, tx_grad, rx_both, rx_grad, firsts, turned, tx_out, rx_out, v_part,
    load_sem, table_sem, store_sem, perm_sem, send_sem, recv_sem,
):
    me = lax.axis_index("ctx")
    section = lax.axis_index("section")
    x, y, z = me // 32, (me // 8) % 4, me % 8

    def peer(i):
        px, py, pz = (x + i // 32) % 2, (y + (i // 8) % 4) % 4, (z + i % 8) % 8
        return px * 32 + py * 8 + pz

    loads = [
        pltpu.make_async_copy(src, dst, load_sem.at[i])
        for i, (src, dst) in enumerate(
            [(conv_input, v_in), (long_filter, v_fi), (gate, v_gate), (saved_conv, v_saved)]
        )
    ]
    for load in loads:
        load.start()
    table_loads = [
        pltpu.make_async_copy(src, dst, table_sem.at[i])
        for i, (src, dst) in enumerate(
            [(outer_fwd_h, outer_fwd), (twist_h, twist), (turn_h, turn), (outer_inv_h, outer_inv)]
        )
    ]

    barrier = pltpu.get_barrier_semaphore()

    def greet(i, carry):
        pl.semaphore_signal(barrier, inc=1, device_id={"ctx": peer(i)}, device_id_type=MESH)
        return carry

    pl.semaphore_signal(barrier, inc=1, device_id={"section": (section + 1) % 4}, device_id_type=MESH)
    lax.fori_loop(1, N_CTX, greet, 0)

    loads[0].wait()
    loads[1].wait()
    pack_signal(v_in, tx_both.at[0], 0, 0)
    pack_signal(v_fi, tx_both.at[0], 0, 32)
    pl.semaphore_wait(barrier, N_CTX)

    passed = pltpu.make_async_remote_copy(
        src_ref=grad_next, dst_ref=v_grad, send_sem=perm_sem.at[0], recv_sem=perm_sem.at[1],
        device_id={"section": (section + 3) % 4}, device_id_type=MESH,
    )
    passed.start()

    def send(tx, rx, which):
        pltpu.make_async_copy(tx.at[me], rx.at[me], recv_sem.at[which]).start()

        def body(i, carry):
            d = peer(i)
            pltpu.make_async_remote_copy(
                src_ref=tx.at[d], dst_ref=rx.at[me], send_sem=send_sem.at[which], recv_sem=recv_sem.at[which],
                device_id={"ctx": d}, device_id_type=MESH,
            ).start()
            return carry

        lax.fori_loop(1, N_CTX, body, 0)

    def arrived(rx, which):
        pltpu.make_async_copy(rx, rx, recv_sem.at[which]).wait()

    def sent(tx, which):
        part = tx.at[pl.ds(0, N_CTX - 1)]
        pltpu.make_async_copy(part, part, send_sem.at[which]).wait()

    send(tx_both.at[0], rx_both.at[0], 0)
    for load in table_loads:
        load.start()
    pack_signal(v_in, tx_both.at[1], 1, 0)
    pack_signal(v_fi, tx_both.at[1], 1, 32)
    loads[2].wait()
    loads[3].wait()
    passed.wait_recv()

    def gating(r, carry):
        rows = pl.ds(pl.multiple_of(r * 16, 16), 16)
        grad = v_grad[rows, :].astype(F32)
        v_gc[rows, :] = (grad * v_gate[rows, :].astype(F32)).astype(BF16)
        v_gg[rows, :] = (grad * v_saved[rows, :].astype(F32)).astype(BF16)
        return carry

    lax.fori_loop(0, BLOCK // 16, gating, 0)
    pack_signal(v_gc, tx_grad.at[0], 0, 0)
    send(tx_grad.at[0], rx_grad.at[0], 1)
    send(tx_both.at[1], rx_both.at[1], 2)
    pack_signal(v_gc, tx_grad.at[1], 1, 0)
    send(tx_grad.at[1], rx_grad.at[1], 3)
    stores = [pltpu.make_async_copy(v_gg, gg_out, store_sem.at[0])]
    stores[0].start()
    for load in table_loads:
        load.wait()

    for half in range(2):
        arrived(rx_both.at[half], 2 * half)
        arrived(rx_grad.at[half], 2 * half + 1)
        first_pass(rx_both.at[half], rx_grad.at[half], outer_fwd, firsts)
        middle_passes(firsts, twist, turn, turned)
        last_pass(turned, outer_inv, tx_out.at[half])
        send(tx_out.at[half], (rx_out, got)[half], 4 + half)

    arrived(rx_out, 4)
    unpack_outputs(rx_out, v_part.at[0], v_part.at[1], 0, 16)
    stores.append(pltpu.make_async_copy(v_part, part_out, store_sem.at[1]))
    stores[1].start()
    arrived(got, 5)

    passed.wait_send()
    for half in range(2):
        sent(tx_both.at[half], 2 * half)
        sent(tx_grad.at[half], 2 * half + 1)
        sent(tx_out.at[half], 4 + half)
    for store in stores:
        store.wait()


def finish(
    gg, part, got, grad_input, grad_gate, filter_grad, v_got, v_gg, v_fi, v_in, load_sem, gg_sem, part_sem, store_sem
):
    loads = [
        pltpu.make_async_copy(got.at[pl.ds(16 * c, 16)], v_got.at[pl.ds(16 * c, 16)], load_sem.at[c]) for c in range(4)
    ]
    gg_loads = [
        pltpu.make_async_copy(gg.at[pl.ds(64 * r, 64)], v_gg.at[pl.ds(64 * r, 64)], gg_sem.at[r]) for r in range(2)
    ]
    part_loads = [
        pltpu.make_async_copy(part.at[i], v.at[:, pl.ds(0, HALF)], part_sem.at[i]) for i, v in enumerate((v_fi, v_in))
    ]
    for copy in loads + gg_loads + part_loads:
        copy.start()
    stores = []

    def store(src, out):
        stores.append(pltpu.make_async_copy(src, out, store_sem.at[len(stores)]))
        stores[-1].start()

    for c in range(4):
        loads[c].wait()
        unpack_outputs(
            v_got.at[pl.ds(16 * c, 16)], v_fi.at[:, pl.ds(HALF + 512 * c, 512)],
            v_in.at[:, pl.ds(HALF + 512 * c, 512)], 0, 4,
        )
        for src, out in ((v_fi, filter_grad), (v_in, grad_input)):
            cols = pl.ds(HALF + 512 * c, 512)
            store(src.at[:, cols], out.at[:, cols])
        if c < 2:
            gg_loads[c].wait()
            store(v_gg.at[pl.ds(64 * c, 64)], grad_gate.at[pl.ds(64 * c, 64)])
        else:
            part_loads[c - 2].wait()
            src, out = ((v_fi, filter_grad), (v_in, grad_input))[c - 2]
            store(src.at[:, pl.ds(0, HALF)], out.at[:, pl.ds(0, HALF)])
    for copy in stores:
        copy.wait()


def per_device(consts, grad_next, gate, conv_input, saved_conv, long_filter):
    args = [a[0] for a in (grad_next, gate, conv_input, saved_conv, long_filter)]
    shard = jax.ShapeDtypeStruct((BLOCK, CHANNELS), BF16)
    any_spec = pl.BlockSpec(memory_space=pl.ANY)
    vmem = lambda *shape: pltpu.VMEM(shape, BF16)
    outs = pl.pallas_call(
        kernel,
        out_shape=[
            shard, jax.ShapeDtypeStruct((2, BLOCK, HALF), BF16), jax.ShapeDtypeStruct((N_CTX, 64, 128), BF16)
        ],
        in_specs=[any_spec] * 9,
        out_specs=[any_spec] * 3,
        scratch_shapes=[vmem(BLOCK, CHANNELS)] * 7
        + [vmem(*c.shape) for c in consts]
        + [
            vmem(2, N_CTX, 64, 128), vmem(2, N_CTX, 32, 128),
            vmem(2, N_CTX, 64, 128), vmem(2, N_CTX, 32, 128),
            vmem(2 * SLOTS, BLOCK, 128), vmem(2 * SLOTS, 64, 128),
            vmem(2, N_CTX, 64, 128), vmem(N_CTX, 64, 128), vmem(2, BLOCK, HALF),
            pltpu.SemaphoreType.DMA((4,)), pltpu.SemaphoreType.DMA((4,)), pltpu.SemaphoreType.DMA((2,)),
            pltpu.SemaphoreType.DMA((2,)), pltpu.SemaphoreType.DMA((6,)), pltpu.SemaphoreType.DMA((6,)),
        ],
        compiler_params=pltpu.CompilerParams(
            collective_id=0, has_side_effects=True, vmem_limit_bytes=58 * 2**20
        ),
    )(*args, *consts)
    outs = pl.pallas_call(
        finish,
        out_shape=[shard] * 3,
        in_specs=[any_spec] * 3,
        out_specs=[any_spec] * 3,
        scratch_shapes=[
            vmem(N_CTX, 64, 128), vmem(BLOCK, CHANNELS), vmem(BLOCK, CHANNELS), vmem(BLOCK, CHANNELS),
            pltpu.SemaphoreType.DMA((4,)), pltpu.SemaphoreType.DMA((2,)),
            pltpu.SemaphoreType.DMA((2,)), pltpu.SemaphoreType.DMA((12,)),
        ],
    )(*outs)
    return tuple(o[None] for o in outs)


def solution(mesh):
    consts = tables()
    spec = P("section", "ctx", None)
    return jax.shard_map(
        functools.partial(per_device, [jnp.asarray(c) for c in consts]),
        mesh=mesh, in_specs=(spec,) * 5, out_specs=(spec,) * 3, check_vma=False,
    )
```

```python
import functools
import math

import jax
import jax.numpy as jnp
import numpy as np
from jax import lax
from jax.experimental import pallas as pl
from jax.experimental.pallas import tpu as pltpu
from jax.sharding import PartitionSpec as P

MESH = pl.DeviceIdType.MESH
BF16 = jnp.bfloat16
F32 = jnp.float32

N_CTX = 64
BLOCK = 128
CHANNELS = 4096
HALF = CHANNELS // 2
WIDTH = HALF // N_CTX
OUTER = 2 * N_CTX
FULL = OUTER * BLOCK
SLOTS = N_CTX


def tables():
    k1 = np.arange(N_CTX + 1, dtype=np.int32)
    at = np.arange(N_CTX, dtype=np.int32)
    step = np.float32(2.0 * math.pi / OUTER)
    angle = step * ((k1[:, None] * at[None, :]) % OUTER).astype(np.float32)
    cos = np.cos(angle).astype(jnp.bfloat16).astype(np.float32)
    sin = (-np.sin(angle)).astype(jnp.bfloat16).astype(np.float32)
    rows = np.stack([cos[:N_CTX], sin[:N_CTX]], axis=1)
    rows[0, 1] = cos[N_CTX]
    weight = np.full((SLOTS, 2, 1), 2.0 / FULL, np.float32)
    weight[0] = 1.0 / FULL
    eye = np.eye(8, dtype=np.float32)
    outer_fwd = np.kron(rows.reshape(2 * SLOTS, N_CTX), eye)
    outer_inv = np.kron((rows * weight).reshape(2 * SLOTS, N_CTX).T, eye)
    j = np.arange(BLOCK, dtype=np.int32)
    freq = k1[:, None, None] + OUTER * j[None, :, None]
    step = np.float32(2.0 * math.pi / FULL)
    angle = step * ((j[None, None, :] * freq) % FULL).astype(np.float32)
    re, im = np.cos(angle), -np.sin(angle)
    top = np.concatenate([re, -im], axis=2)
    low = np.concatenate([im, re], axis=2)
    twist = np.concatenate([top, low], axis=1)
    twist[0, :, BLOCK:] = 0.0
    twist[N_CTX] = np.concatenate([np.zeros((2 * BLOCK, BLOCK)), np.concatenate([re[N_CTX], im[N_CTX]], axis=0)], axis=1)
    turn = twist.transpose(0, 2, 1)
    return [t.astype(jnp.bfloat16) for t in (outer_fwd, outer_inv, twist, turn)]


def lane_group(shape):
    return lax.broadcasted_iota(jnp.int32, shape, len(shape) - 1) // WIDTH


def pick(groups, parts):
    out = parts[3]
    for g in (2, 1, 0):
        out = jnp.where(groups == g, parts[g], out)
    return out


def rolled(value, shift):
    return value if isinstance(shift, int) and shift % 128 == 0 else pltpu.roll(value, shift % 128 if isinstance(shift, int) else shift, 1)


def pack_signal(src, dst, half, row):
    groups = lane_group((32, 128))

    def body(e, carry):
        cols = pl.ds(pl.multiple_of(half * HALF + e * 128, 128), 128)
        quarters = [src[32 * q : 32 * q + 32, cols] for q in range(4)]
        for g in range(4):
            parts = [rolled(quarters[q], 32 * (q - g)) for q in range(4)]
            dst[4 * e + g, row : row + 32, :] = pick(groups, parts)
        return carry

    lax.fori_loop(0, 16, body, 0, unroll=4)


def unpack_outputs(src, filter_out, input_out, first, last):
    groups = lane_group((64, 128))

    def body(e, carry):
        cols = pl.ds(pl.multiple_of(e * 128, 128), 128)
        got = [src[4 * e + g] for g in range(4)]
        for at in range(4):
            parts = [rolled(got[g], 32 * (g - at)) for g in range(4)]
            out = (filter_out, input_out)[at % 2]
            out[64 * (at // 2) : 64 * (at // 2) + 64, cols] = pick(groups, parts)
        return carry

    lax.fori_loop(first, last, body, 0, unroll=4)


def first_pass(both, grad, outer_fwd, firsts):
    groups = lane_group((N_CTX * 16, 128))

    def body(jb, carry):
        q = jb // 2
        row = pl.multiple_of((jb % 2) * 16, 16)
        take = lambda ref, at: ref[:, pl.ds(at, 16), :].astype(F32).reshape(N_CTX * 16, 128)
        x_in, x_fi, x_gr = take(both, row), take(both, row + 32), take(grad, row)
        shift = 128 - 32 * q
        parts = [
            pltpu.roll(x_in, shift % 128, 1),
            pltpu.roll(x_fi, (shift + 32) % 128, 1),
            pltpu.roll(x_gr, (shift + 64) % 128, 1),
            pltpu.roll(x_gr, (shift + 96) % 128, 1),
        ]
        x = pick(groups, parts).reshape(N_CTX, 16, 128)
        x = jnp.concatenate(
            [x[:, 8 * h : 8 * h + 8].reshape(N_CTX * 8, 128).astype(BF16) for h in range(2)], axis=1
        )
        for mb in range(2):
            y = jnp.dot(outer_fwd[512 * mb : 512 * mb + 512, :], x, preferred_element_type=F32)
            y = jnp.concatenate([y[:, 128 * h : 128 * h + 128].reshape(64, 8, 128) for h in range(2)], axis=1)
            firsts[64 * mb : 64 * mb + 64, pl.ds(pl.multiple_of(jb * 16, 16), 16), :] = y.astype(BF16)
        return carry

    lax.fori_loop(0, 8, body, 0)


def middle_passes(firsts, twist, turn, turned):
    low = lax.broadcasted_iota(jnp.int32, (64, 128), 1) < 64

    def spectra(k1, slot):
        data = firsts[pl.ds(2 * slot, 2)].reshape(2 * BLOCK, 128)
        return jnp.dot(twist[k1], data, preferred_element_type=F32)

    def crossed(spec):
        re, im = spec[:BLOCK], spec[BLOCK:]
        grad_re, grad_im = pltpu.roll(re, 64, 1), pltpu.roll(im, 64, 1)
        return jnp.concatenate(
            [(grad_re * re + grad_im * im).astype(BF16), (grad_im * re - grad_re * im).astype(BF16)], axis=0
        )

    def turn_of(k1, cross):
        return jnp.dot(turn[k1], cross, preferred_element_type=F32)

    def keep(slot, value):
        for part in range(2):
            at = part * BLOCK
            both = jnp.where(low, value[at : at + 64], pltpu.roll(value[at + 64 : at + 128], 64, 1))
            turned[2 * slot + part] = both.astype(BF16)

    def body(i, carry):
        slots = [1 + 7 * i + u for u in range(7)]
        specs = [spectra(k, k) for k in slots]
        cross = [crossed(v) for v in specs]
        turns = [turn_of(k, c) for k, c in zip(slots, cross)]
        for k, t in zip(slots, turns):
            keep(k, t)
        return carry

    keep(0, turn_of(0, crossed(spectra(0, 0))) + turn_of(N_CTX, crossed(spectra(N_CTX, 0))))
    lax.fori_loop(0, 9, body, 0)


def last_pass(turned, outer_inv, out):
    def body(jb, carry):
        rows = pl.ds(pl.multiple_of(jb * 16, 16), 16)
        t = turned[:, rows, :].astype(F32)
        t = jnp.concatenate(
            [t[:, 8 * h : 8 * h + 8].reshape(2 * SLOTS * 8, 128).astype(BF16) for h in range(2)], axis=1
        )
        y = jnp.dot(outer_inv[...], t, preferred_element_type=F32)
        y = jnp.concatenate([y[:, 128 * h : 128 * h + 128].reshape(N_CTX, 8, 128) for h in range(2)], axis=1)
        out[:, rows, :] = y.astype(BF16)
        return carry

    lax.fori_loop(0, 4, body, 0)


def kernel(
    grad_next, gate, conv_input, saved_conv, long_filter, outer_fwd_h, outer_inv_h, twist_h, turn_h,
    v_gg, v_part, got,
    v_in, v_fi, v_gate, v_saved, v_grad, v_gc, outer_fwd, outer_inv, twist, turn,
    tx_both, tx_grad, rx_both, rx_grad, firsts, turned, tx_out, rx_out,
    load_sem, table_sem, perm_sem, send_sem, recv_sem,
):
    me = lax.axis_index("ctx")
    section = lax.axis_index("section")
    x, y, z = me // 32, (me // 8) % 4, me % 8

    def peer(i):
        px, py, pz = (x + i // 32) % 2, (y + (i // 8) % 4) % 4, (z + i % 8) % 8
        return px * 32 + py * 8 + pz

    loads = [
        pltpu.make_async_copy(src, dst, load_sem.at[i])
        for i, (src, dst) in enumerate(
            [(conv_input, v_in), (long_filter, v_fi), (gate, v_gate), (saved_conv, v_saved)]
        )
    ]
    for load in loads:
        load.start()
    table_loads = [
        pltpu.make_async_copy(src, dst, table_sem.at[i])
        for i, (src, dst) in enumerate(
            [(outer_fwd_h, outer_fwd), (twist_h, twist), (turn_h, turn), (outer_inv_h, outer_inv)]
        )
    ]

    barrier = pltpu.get_barrier_semaphore()

    def greet(i, carry):
        pl.semaphore_signal(barrier, inc=1, device_id={"ctx": peer(i)}, device_id_type=MESH)
        return carry

    pl.semaphore_signal(barrier, inc=1, device_id={"section": (section + 1) % 4}, device_id_type=MESH)
    lax.fori_loop(1, N_CTX, greet, 0)

    loads[0].wait()
    loads[1].wait()
    pack_signal(v_in, tx_both.at[0], 0, 0)
    pack_signal(v_fi, tx_both.at[0], 0, 32)
    pl.semaphore_wait(barrier, N_CTX)

    def pass_along(piece):
        half = piece // 8
        at = (pl.ds(pl.multiple_of(piece % 8 * 16, 16), 16), pl.ds(pl.multiple_of(half * HALF, HALF), HALF))
        pltpu.make_async_remote_copy(
            src_ref=grad_next.at[at], dst_ref=v_grad.at[at], send_sem=perm_sem.at[half], recv_sem=perm_sem.at[2 + half],
            device_id={"section": (section + 3) % 4}, device_id_type=MESH,
        ).start()

    def passed(half, which):
        part = v_grad.at[:, pl.ds(half * HALF, HALF)]
        pltpu.make_async_copy(part, part, perm_sem.at[which]).wait()

    def send(tx, rx, which, beside=False):
        pltpu.make_async_copy(tx.at[me], rx.at[me], recv_sem.at[which]).start()

        def body(i, carry):
            d = peer(i)
            pltpu.make_async_remote_copy(
                src_ref=tx.at[d], dst_ref=rx.at[me], send_sem=send_sem.at[which], recv_sem=recv_sem.at[which],
                device_id={"ctx": d}, device_id_type=MESH,
            ).start()
            if beside:

                @pl.when(i % 4 == 1)
                def _():
                    pass_along(i // 4)

            return carry

        lax.fori_loop(1, N_CTX, body, 0)

    def arrived(rx, which):
        pltpu.make_async_copy(rx, rx, recv_sem.at[which]).wait()

    def sent(tx, which):
        part = tx.at[pl.ds(0, N_CTX - 1)]
        pltpu.make_async_copy(part, part, send_sem.at[which]).wait()

    send(tx_both.at[0], rx_both.at[0], 0, beside=True)
    for load in table_loads:
        load.start()
    pack_signal(v_in, tx_both.at[1], 1, 0)
    pack_signal(v_fi, tx_both.at[1], 1, 32)
    loads[2].wait()
    loads[3].wait()

    def gating(half):
        cols = pl.ds(half * HALF, HALF)

        def body(r, carry):
            rows = pl.ds(pl.multiple_of(r * 16, 16), 16)
            grad = v_grad[rows, cols].astype(F32)
            v_gc[rows, cols] = (grad * v_gate[rows, cols].astype(F32)).astype(BF16)
            v_gg[rows, cols] = (grad * v_saved[rows, cols].astype(F32)).astype(BF16)
            return carry

        lax.fori_loop(0, BLOCK // 16, body, 0)

    passed(0, 2)
    gating(0)
    pack_signal(v_gc, tx_grad.at[0], 0, 0)
    send(tx_grad.at[0], rx_grad.at[0], 1)
    send(tx_both.at[1], rx_both.at[1], 2)
    passed(1, 3)
    gating(1)
    pack_signal(v_gc, tx_grad.at[1], 1, 0)
    send(tx_grad.at[1], rx_grad.at[1], 3)
    for load in table_loads:
        load.wait()

    for half in range(2):
        arrived(rx_both.at[half], 2 * half)
        arrived(rx_grad.at[half], 2 * half + 1)
        first_pass(rx_both.at[half], rx_grad.at[half], outer_fwd, firsts)
        middle_passes(firsts, twist, turn, turned)
        last_pass(turned, outer_inv, tx_out.at[half])
        send(tx_out.at[half], (rx_out, got)[half], 4 + half)

    arrived(rx_out, 4)
    unpack_outputs(rx_out, v_part.at[0], v_part.at[1], 0, 16)
    arrived(got, 5)

    passed(0, 0)
    passed(1, 1)
    for half in range(2):
        sent(tx_both.at[half], 2 * half)
        sent(tx_grad.at[half], 2 * half + 1)
        sent(tx_out.at[half], 4 + half)


def finish(gg, part, got, grad_input, grad_gate, filter_grad, v_fi, v_in, store_sem):
    stores = []

    def store(src, out):
        stores.append(pltpu.make_async_copy(src, out, store_sem.at[len(stores)]))
        stores[-1].start()

    store(gg, grad_gate)
    for i, out in enumerate((filter_grad, grad_input)):
        store(part.at[i], out.at[:, pl.ds(0, HALF)])
    for c in range(4):
        cols = pl.ds(512 * c, 512)
        unpack_outputs(got.at[pl.ds(16 * c, 16)], v_fi.at[:, cols], v_in.at[:, cols], 0, 4)
        for src, out in ((v_fi, filter_grad), (v_in, grad_input)):
            store(src.at[:, cols], out.at[:, pl.ds(HALF + 512 * c, 512)])
    for copy in stores:
        copy.wait()


def per_device(consts, grad_next, gate, conv_input, saved_conv, long_filter):
    args = [a[0] for a in (grad_next, gate, conv_input, saved_conv, long_filter)]
    shard = jax.ShapeDtypeStruct((BLOCK, CHANNELS), BF16)
    any_spec = pl.BlockSpec(memory_space=pl.ANY)
    vmem_spec = pl.BlockSpec(memory_space=pltpu.VMEM)
    vmem = lambda *shape: pltpu.VMEM(shape, BF16)
    outs = pl.pallas_call(
        kernel,
        out_shape=[vmem(BLOCK, CHANNELS), vmem(2, BLOCK, HALF), vmem(N_CTX, 64, 128)],
        in_specs=[any_spec] * 9,
        out_specs=[vmem_spec] * 3,
        scratch_shapes=[vmem(BLOCK, CHANNELS)] * 6
        + [vmem(*c.shape) for c in consts]
        + [
            vmem(2, N_CTX, 64, 128), vmem(2, N_CTX, 32, 128),
            vmem(2, N_CTX, 64, 128), vmem(2, N_CTX, 32, 128),
            vmem(2 * SLOTS, BLOCK, 128), vmem(2 * SLOTS, 64, 128),
            vmem(2, N_CTX, 64, 128), vmem(N_CTX, 64, 128),
            pltpu.SemaphoreType.DMA((4,)), pltpu.SemaphoreType.DMA((4,)),
            pltpu.SemaphoreType.DMA((4,)), pltpu.SemaphoreType.DMA((6,)), pltpu.SemaphoreType.DMA((6,)),
        ],
        compiler_params=pltpu.CompilerParams(
            collective_id=0, has_side_effects=True, vmem_limit_bytes=50 * 2**20
        ),
    )(*args, *consts)
    outs = pl.pallas_call(
        finish,
        out_shape=[shard] * 3,
        in_specs=[vmem_spec] * 3,
        out_specs=[any_spec] * 3,
        scratch_shapes=[vmem(BLOCK, HALF), vmem(BLOCK, HALF), pltpu.SemaphoreType.DMA((11,))],
        compiler_params=pltpu.CompilerParams(vmem_limit_bytes=12 * 2**20),
    )(*outs)
    return tuple(o[None] for o in outs)


def solution(mesh):
    consts = tables()
    spec = P("section", "ctx", None)
    return jax.shard_map(
        functools.partial(per_device, [jnp.asarray(c) for c in consts]),
        mesh=mesh, in_specs=(spec,) * 5, out_specs=(spec,) * 3, check_vma=False,
    )
```

```python
import functools
import math

import jax
import jax.numpy as jnp
import numpy as np
from jax import lax
from jax.experimental import pallas as pl
from jax.experimental.pallas import tpu as pltpu
from jax.sharding import PartitionSpec as P

MESH = pl.DeviceIdType.MESH
BF16 = jnp.bfloat16
F32 = jnp.float32

N_CTX = 64
BLOCK = 128
CHANNELS = 4096
HALF = CHANNELS // 2
WIDTH = HALF // N_CTX
OUTER = 2 * N_CTX
FULL = OUTER * BLOCK
SLOTS = N_CTX


def tables():
    k1 = np.arange(N_CTX + 1, dtype=np.int32)
    at = np.arange(N_CTX, dtype=np.int32)
    step = np.float32(2.0 * math.pi / OUTER)
    angle = step * ((k1[:, None] * at[None, :]) % OUTER).astype(np.float32)
    cos = np.cos(angle).astype(jnp.bfloat16).astype(np.float32)
    sin = (-np.sin(angle)).astype(jnp.bfloat16).astype(np.float32)
    rows = np.stack([cos[:N_CTX], sin[:N_CTX]], axis=1)
    rows[0, 1] = cos[N_CTX]
    weight = np.full((SLOTS, 2, 1), 2.0 / FULL, np.float32)
    weight[0] = 1.0 / FULL
    eye = np.eye(8, dtype=np.float32)
    outer_fwd = np.kron(rows.reshape(2 * SLOTS, N_CTX), eye)
    outer_inv = np.kron((rows * weight).reshape(2 * SLOTS, N_CTX).T, eye)
    j = np.arange(BLOCK, dtype=np.int32)
    freq = k1[:, None, None] + OUTER * j[None, :, None]
    step = np.float32(2.0 * math.pi / FULL)
    angle = step * ((j[None, None, :] * freq) % FULL).astype(np.float32)
    re, im = np.cos(angle), -np.sin(angle)
    top = np.concatenate([re, -im], axis=2)
    low = np.concatenate([im, re], axis=2)
    twist = np.concatenate([top, low], axis=1)
    twist[0, :, BLOCK:] = 0.0
    twist[N_CTX] = np.concatenate([np.zeros((2 * BLOCK, BLOCK)), np.concatenate([re[N_CTX], im[N_CTX]], axis=0)], axis=1)
    turn = twist.transpose(0, 2, 1)
    return [t.astype(jnp.bfloat16) for t in (outer_fwd, outer_inv, twist, turn)]


def lane_group(shape):
    return lax.broadcasted_iota(jnp.int32, shape, len(shape) - 1) // WIDTH


def pick(groups, parts):
    out = parts[3]
    for g in (2, 1, 0):
        out = jnp.where(groups == g, parts[g], out)
    return out


def rolled(value, shift):
    return value if isinstance(shift, int) and shift % 128 == 0 else pltpu.roll(value, shift % 128 if isinstance(shift, int) else shift, 1)


def pack_signal(src, dst, half, row):
    groups = lane_group((32, 128))

    def body(e, carry):
        cols = pl.ds(pl.multiple_of(half * HALF + e * 128, 128), 128)
        quarters = [src[32 * q : 32 * q + 32, cols] for q in range(4)]
        for g in range(4):
            parts = [rolled(quarters[q], 32 * (q - g)) for q in range(4)]
            dst[4 * e + g, row : row + 32, :] = pick(groups, parts)
        return carry

    lax.fori_loop(0, 16, body, 0, unroll=4)


def unpack_outputs(src, filter_out, input_out, first, last):
    groups = lane_group((64, 128))

    def body(e, carry):
        cols = pl.ds(pl.multiple_of(e * 128, 128), 128)
        got = [src[4 * e + g] for g in range(4)]
        for at in range(4):
            parts = [rolled(got[g], 32 * (g - at)) for g in range(4)]
            out = (filter_out, input_out)[at % 2]
            out[64 * (at // 2) : 64 * (at // 2) + 64, cols] = pick(groups, parts)
        return carry

    lax.fori_loop(first, last, body, 0, unroll=4)


def first_pass(both, grad, outer_fwd, firsts):
    groups = lane_group((N_CTX * 16, 128))

    def body(jb, carry):
        q = jb // 2
        row = pl.multiple_of((jb % 2) * 16, 16)
        take = lambda ref, at: ref[:, pl.ds(at, 16), :].astype(F32).reshape(N_CTX * 16, 128)
        x_in, x_fi, x_gr = take(both, row), take(both, row + 32), take(grad, row)
        shift = 128 - 32 * q
        parts = [
            pltpu.roll(x_in, shift % 128, 1),
            pltpu.roll(x_fi, (shift + 32) % 128, 1),
            pltpu.roll(x_gr, (shift + 64) % 128, 1),
            pltpu.roll(x_gr, (shift + 96) % 128, 1),
        ]
        x = pick(groups, parts).reshape(N_CTX, 16, 128)
        x = jnp.concatenate(
            [x[:, 8 * h : 8 * h + 8].reshape(N_CTX * 8, 128).astype(BF16) for h in range(2)], axis=1
        )
        for mb in range(2):
            y = jnp.dot(outer_fwd[512 * mb : 512 * mb + 512, :], x, preferred_element_type=F32)
            y = jnp.concatenate([y[:, 128 * h : 128 * h + 128].reshape(64, 8, 128) for h in range(2)], axis=1)
            firsts[64 * mb : 64 * mb + 64, pl.ds(pl.multiple_of(jb * 16, 16), 16), :] = y.astype(BF16)
        return carry

    lax.fori_loop(0, 8, body, 0)


def middle_passes(firsts, twist, turn, turned):
    low = lax.broadcasted_iota(jnp.int32, (64, 128), 1) < 64

    def spectra(k1, slot):
        data = firsts[pl.ds(2 * slot, 2)].reshape(2 * BLOCK, 128)
        return jnp.dot(twist[k1], data, preferred_element_type=F32)

    def crossed(spec):
        re, im = spec[:BLOCK], spec[BLOCK:]
        grad_re, grad_im = pltpu.roll(re, 64, 1), pltpu.roll(im, 64, 1)
        return jnp.concatenate(
            [(grad_re * re + grad_im * im).astype(BF16), (grad_im * re - grad_re * im).astype(BF16)], axis=0
        )

    def turn_of(k1, cross):
        return jnp.dot(turn[k1], cross, preferred_element_type=F32)

    def keep(slot, value):
        for part in range(2):
            at = part * BLOCK
            both = jnp.where(low, value[at : at + 64], pltpu.roll(value[at + 64 : at + 128], 64, 1))
            turned[2 * slot + part] = both.astype(BF16)

    def body(i, carry):
        slots = [1 + 7 * i + u for u in range(7)]
        specs = [spectra(k, k) for k in slots]
        cross = [crossed(v) for v in specs]
        turns = [turn_of(k, c) for k, c in zip(slots, cross)]
        for k, t in zip(slots, turns):
            keep(k, t)
        return carry

    keep(0, turn_of(0, crossed(spectra(0, 0))) + turn_of(N_CTX, crossed(spectra(N_CTX, 0))))
    lax.fori_loop(0, 9, body, 0)


def last_pass(turned, outer_inv, out):
    def body(jb, carry):
        rows = pl.ds(pl.multiple_of(jb * 16, 16), 16)
        t = turned[:, rows, :].astype(F32)
        t = jnp.concatenate(
            [t[:, 8 * h : 8 * h + 8].reshape(2 * SLOTS * 8, 128).astype(BF16) for h in range(2)], axis=1
        )
        y = jnp.dot(outer_inv[...], t, preferred_element_type=F32)
        y = jnp.concatenate([y[:, 128 * h : 128 * h + 128].reshape(N_CTX, 8, 128) for h in range(2)], axis=1)
        out[:, rows, :] = y.astype(BF16)
        return carry

    lax.fori_loop(0, 4, body, 0)


def kernel(
    grad_next, gate, conv_input, saved_conv, long_filter, outer_fwd_h, outer_inv_h, twist_h, turn_h,
    v_gg, v_part, got,
    v_in, v_fi, v_gate, v_saved, v_grad, v_gc, outer_fwd, outer_inv, twist, turn,
    tx_both, tx_grad, rx_both, rx_grad, firsts, turned, tx_out, rx_out,
    load_sem, table_sem, perm_sem, send_sem, recv_sem,
):
    me = lax.axis_index("ctx")
    section = lax.axis_index("section")
    x, y, z = me // 32, (me // 8) % 4, me % 8

    def peer(i):
        px, py, pz = (x + i // 32) % 2, (y + (i // 8) % 4) % 4, (z + i % 8) % 8
        return px * 32 + py * 8 + pz

    first, second = pl.ds(0, HALF), pl.ds(HALF, HALF)
    loads = [
        pltpu.make_async_copy(src, dst, load_sem.at[i])
        for i, (src, dst) in enumerate(
            [
                (conv_input.at[:, first], v_in.at[:, first]), (long_filter.at[:, first], v_fi.at[:, first]),
                (conv_input.at[:, second], v_in.at[:, second]), (long_filter.at[:, second], v_fi.at[:, second]),
                (gate, v_gate), (saved_conv, v_saved),
            ]
        )
    ]
    for load in loads[:2]:
        load.start()
    table_loads = [
        pltpu.make_async_copy(src, dst, table_sem.at[i])
        for i, (src, dst) in enumerate(
            [(outer_fwd_h, outer_fwd), (twist_h, twist), (turn_h, turn), (outer_inv_h, outer_inv)]
        )
    ]

    barrier = pltpu.get_barrier_semaphore()

    def greet(i, carry):
        pl.semaphore_signal(barrier, inc=1, device_id={"ctx": peer(i)}, device_id_type=MESH)
        return carry

    pl.semaphore_signal(barrier, inc=1, device_id={"section": (section + 1) % 4}, device_id_type=MESH)
    lax.fori_loop(1, N_CTX, greet, 0)

    loads[0].wait()
    pack_signal(v_in, tx_both.at[0], 0, 0)
    loads[1].wait()
    for load in loads[2:]:
        load.start()
    pack_signal(v_fi, tx_both.at[0], 0, 32)
    pl.semaphore_wait(barrier, N_CTX)

    def pass_along(piece):
        half = piece // 8
        at = (pl.ds(pl.multiple_of(piece % 8 * 16, 16), 16), pl.ds(pl.multiple_of(half * HALF, HALF), HALF))
        pltpu.make_async_remote_copy(
            src_ref=grad_next.at[at], dst_ref=v_grad.at[at], send_sem=perm_sem.at[half], recv_sem=perm_sem.at[2 + half],
            device_id={"section": (section + 3) % 4}, device_id_type=MESH,
        ).start()

    def passed(half, which):
        part = v_grad.at[:, pl.ds(half * HALF, HALF)]
        pltpu.make_async_copy(part, part, perm_sem.at[which]).wait()

    def send(tx, rx, which, beside=False):
        pltpu.make_async_copy(tx.at[me], rx.at[me], recv_sem.at[which]).start()

        def body(i, carry):
            d = peer(i)
            pltpu.make_async_remote_copy(
                src_ref=tx.at[d], dst_ref=rx.at[me], send_sem=send_sem.at[which], recv_sem=recv_sem.at[which],
                device_id={"ctx": d}, device_id_type=MESH,
            ).start()
            if beside:

                @pl.when(i % 4 == 1)
                def _():
                    pass_along(i // 4)

            return carry

        lax.fori_loop(1, N_CTX, body, 0)

    def arrived(rx, which):
        pltpu.make_async_copy(rx, rx, recv_sem.at[which]).wait()

    def sent(tx, which):
        part = tx.at[pl.ds(0, N_CTX - 1)]
        pltpu.make_async_copy(part, part, send_sem.at[which]).wait()

    send(tx_both.at[0], rx_both.at[0], 0, beside=True)
    for load in table_loads:
        load.start()
    for load in loads[2:]:
        load.wait()
    pack_signal(v_in, tx_both.at[1], 1, 0)
    pack_signal(v_fi, tx_both.at[1], 1, 32)

    def gating(half):
        cols = pl.ds(half * HALF, HALF)

        def body(r, carry):
            rows = pl.ds(pl.multiple_of(r * 16, 16), 16)
            grad = v_grad[rows, cols].astype(F32)
            v_gc[rows, cols] = (grad * v_gate[rows, cols].astype(F32)).astype(BF16)
            v_gg[rows, cols] = (grad * v_saved[rows, cols].astype(F32)).astype(BF16)
            return carry

        lax.fori_loop(0, BLOCK // 16, body, 0)

    passed(0, 2)
    gating(0)
    pack_signal(v_gc, tx_grad.at[0], 0, 0)
    send(tx_grad.at[0], rx_grad.at[0], 1)
    send(tx_both.at[1], rx_both.at[1], 2)
    passed(1, 3)
    gating(1)
    pack_signal(v_gc, tx_grad.at[1], 1, 0)
    send(tx_grad.at[1], rx_grad.at[1], 3)
    for load in table_loads:
        load.wait()

    for half in range(2):
        arrived(rx_both.at[half], 2 * half)
        arrived(rx_grad.at[half], 2 * half + 1)
        first_pass(rx_both.at[half], rx_grad.at[half], outer_fwd, firsts)
        middle_passes(firsts, twist, turn, turned)
        last_pass(turned, outer_inv, tx_out.at[half])
        send(tx_out.at[half], (rx_out, got)[half], 4 + half)

    arrived(rx_out, 4)
    unpack_outputs(rx_out, v_part.at[0], v_part.at[1], 0, 16)
    arrived(got, 5)

    passed(0, 0)
    passed(1, 1)
    for half in range(2):
        sent(tx_both.at[half], 2 * half)
        sent(tx_grad.at[half], 2 * half + 1)
        sent(tx_out.at[half], 4 + half)


def finish(gg, part, got, grad_input, grad_gate, filter_grad, v_fi, v_in, store_sem):
    stores = []

    def store(src, out):
        stores.append(pltpu.make_async_copy(src, out, store_sem.at[len(stores)]))
        stores[-1].start()

    store(gg, grad_gate)
    for i, out in enumerate((filter_grad, grad_input)):
        store(part.at[i], out.at[:, pl.ds(0, HALF)])
    for c in range(4):
        cols = pl.ds(512 * c, 512)
        unpack_outputs(got.at[pl.ds(16 * c, 16)], v_fi.at[:, cols], v_in.at[:, cols], 0, 4)
        for src, out in ((v_fi, filter_grad), (v_in, grad_input)):
            store(src.at[:, cols], out.at[:, pl.ds(HALF + 512 * c, 512)])
    for copy in stores:
        copy.wait()


def per_device(consts, grad_next, gate, conv_input, saved_conv, long_filter):
    args = [a[0] for a in (grad_next, gate, conv_input, saved_conv, long_filter)]
    shard = jax.ShapeDtypeStruct((BLOCK, CHANNELS), BF16)
    any_spec = pl.BlockSpec(memory_space=pl.ANY)
    vmem_spec = pl.BlockSpec(memory_space=pltpu.VMEM)
    vmem = lambda *shape: pltpu.VMEM(shape, BF16)
    outs = pl.pallas_call(
        kernel,
        out_shape=[vmem(BLOCK, CHANNELS), vmem(2, BLOCK, HALF), vmem(N_CTX, 64, 128)],
        in_specs=[any_spec] * 9,
        out_specs=[vmem_spec] * 3,
        scratch_shapes=[vmem(BLOCK, CHANNELS)] * 6
        + [vmem(*c.shape) for c in consts]
        + [
            vmem(2, N_CTX, 64, 128), vmem(2, N_CTX, 32, 128),
            vmem(2, N_CTX, 64, 128), vmem(2, N_CTX, 32, 128),
            vmem(2 * SLOTS, BLOCK, 128), vmem(2 * SLOTS, 64, 128),
            vmem(2, N_CTX, 64, 128), vmem(N_CTX, 64, 128),
            pltpu.SemaphoreType.DMA((6,)), pltpu.SemaphoreType.DMA((4,)),
            pltpu.SemaphoreType.DMA((4,)), pltpu.SemaphoreType.DMA((6,)), pltpu.SemaphoreType.DMA((6,)),
        ],
        compiler_params=pltpu.CompilerParams(
            collective_id=0, has_side_effects=True, vmem_limit_bytes=50 * 2**20
        ),
    )(*args, *consts)
    outs = pl.pallas_call(
        finish,
        out_shape=[shard] * 3,
        in_specs=[vmem_spec] * 3,
        out_specs=[any_spec] * 3,
        scratch_shapes=[vmem(BLOCK, HALF), vmem(BLOCK, HALF), pltpu.SemaphoreType.DMA((11,))],
        compiler_params=pltpu.CompilerParams(vmem_limit_bytes=12 * 2**20),
    )(*outs)
    return tuple(o[None] for o in outs)


def solution(mesh):
    consts = tables()
    spec = P("section", "ctx", None)
    return jax.shard_map(
        functools.partial(per_device, [jnp.asarray(c) for c in consts]),
        mesh=mesh, in_specs=(spec,) * 5, out_specs=(spec,) * 3, check_vma=False,
    )
```
